128 devices in a mesh: kc: 16 (over x_hi, z, core), ia: 8 (over x_lo, y).
Axes of the slice: x: 4 (x_hi: 2, x_lo: 2; x = x_hi * 2 + x_lo), y: 4, z: 4, core: 2. Of those that a mesh axis runs over, the one named last changes fastest.
Arguments:
- amplitudes: bfloat16 [32768, 32768], P('ia', 'kc'), may hold values from -0.03125 to 0.03125
- occupied_factors: bfloat16 [2048, 4096], P('kc'), may hold values from -0.1875 to 0.1875
- virtual_factors: bfloat16 [2048, 4096], P('kc', 'ia'), may hold values from -6 to 6
Outputs:
- residual: float32 [32768, 512], P('ia', 'kc')
The draws below stay inside these ranges and needn't reach their ends.
All inputs are finite; a program needn't handle non-finite values.
Results may differ from the reference program's by a relative error of at most 0.0029.
Values may be sent and summed in bfloat16 or wider, within the bound.
No kernel may reach another device: no remote copies, remote signals or barrier semaphores. Data moves between devices by JAX's collectives and lax.ppermute only.
A program may use at most 128 MiB of HBM per device.

```python
import jax
import jax.numpy as jnp
from jax import lax

O = 64
V = 512
Q = 2048
BW = 8


def spiked(array, stream_key, source, target, shards_of, factor):
    owner, partner = [(jnp.arange(array.shape[position]) // (array.shape[position] // shards_of)).reshape([-1 if axis == position else 1 for axis in range(array.ndim)]) for position in (source, target)]
    chosen = jax.random.permutation(stream_key, shards_of)[partner]
    strong = (owner == chosen) | (owner == (partner + shards_of // 2) % shards_of)
    return jnp.where(strong, factor * array, array)


def shard_levels(rng, dims, cuts, least, high):
    def one(axis_at, shards_of):
        steps = jax.random.uniform(jax.random.fold_in(jax.random.fold_in(rng, 6), axis_at), (shards_of,), jnp.float32, least / len(cuts), high / len(cuts))
        return jnp.repeat(jnp.exp(steps), dims[axis_at] // shards_of).reshape((-1,) + (1,) * (len(dims) - axis_at - 1))

    gain = one(*cuts[0])
    for cut in cuts[1:]:
        gain = gain * one(*cut)
    return gain


def gaussian(own_key, dims, deviation, most, split=(), held_as=jnp.bfloat16):
    values = jax.random.normal(own_key, dims, jnp.float32) * deviation
    if len(split) > 0:
        values = shard_levels(own_key, dims, split, -0.22, 0.18) * values
    return jnp.clip(values, min=-most, max=most).astype(held_as)


def heavy_noise(own_key, extent, width, bound, pieces, heavy, held_as=jnp.bfloat16):
    entries = width * jax.random.normal(own_key, extent, jnp.float32)
    if pieces:
        entries = entries * shard_levels(own_key, extent, pieces, -0.22, 0.18)
    return jnp.clip(spiked(entries, jax.random.fold_in(own_key, 3), *heavy), -bound, bound).astype(held_as)


def setup_inputs(seed: int = 0) -> dict:
    splits = jax.random.split(jax.random.key(seed), 4)
    return {
        "amplitudes": gaussian(splits[0], (O * V, O * V), (O * V) ** -0.5, 0.03125, ((0, 8), (1, 16))),
        "occupied_factors": heavy_noise(splits[1], (Q, O * O), Q ** -0.5, 0.1875, ((0, 16),), (0, 1, 16, 2.0)),
        "virtual_factors": gaussian(splits[2], (Q, V * BW), 1.0, 6.0, ((0, 16), (1, 8))),
    }


def reference(amplitudes, occupied_factors, virtual_factors):
    integrals = jnp.dot(occupied_factors.T, virtual_factors, preferred_element_type=jnp.float32).astype(jnp.bfloat16)
    cycle_block = integrals.reshape(O, O, V, BW).transpose(0, 2, 1, 3).reshape(O * V, O * BW)

    def one_block(amplitude_rows):
        return jnp.dot(amplitude_rows, cycle_block, preferred_element_type=jnp.float32)

    blocks = lax.map(one_block, amplitudes.reshape(O, V, O * V))
    return blocks.reshape(O * V, O * BW)
```

```python
import functools

import jax
import jax.numpy as jnp
from jax import lax
from jax.experimental import pallas as pl
from jax.experimental.pallas import tpu as pltpu
from jax.sharding import PartitionSpec as P

O = 64
V = 512
BW = 8
F32 = jnp.float32
BF16 = jnp.bfloat16
MIB = 1 << 20


def block_kernel(core_ref, kept_ref, came_ref, out_ref):
    kj, cb = kept_ref.shape
    ks = kj // O
    cs = cb // BW
    rows = O * BW
    integrals = (kept_ref[...] + came_ref[...]).astype(BF16)
    source = lax.broadcasted_iota(jnp.int32, (cb, cb), 0)
    target = lax.broadcasted_iota(jnp.int32, (cb, cb), 1)
    move = jnp.where(source == (target % cs) * BW + target // cs, 1.0, 0.0).astype(BF16)
    by_b = jnp.dot(integrals, move, preferred_element_type=F32).astype(BF16)
    stacked = jnp.concatenate(
        [
            jnp.concatenate(
                [by_b[k * O : (k + 1) * O, b * cs : (b + 1) * cs] for b in range(BW)], axis=0
            )
            for k in range(ks)
        ],
        axis=1,
    )
    half = rows // 2
    target = lax.broadcasted_iota(jnp.int32, (rows, rows), 0)
    source = lax.broadcasted_iota(jnp.int32, (rows, rows), 1)
    core = (core_ref[0] + target // half) % 2
    within = target % half
    j = (within // 32) * 8 + core * 4 + (within % 32) // BW
    move = jnp.where(source == (within % BW) * O + j, 1.0, 0.0).astype(BF16)
    out_ref[...] = jnp.dot(move, stacked, preferred_element_type=F32).astype(BF16)


def cycle_blocks(core, kept, came):
    kj, cb = kept.shape
    return pl.pallas_call(
        block_kernel,
        out_shape=jax.ShapeDtypeStruct((O * BW, kj // O * (cb // BW)), BF16),
        in_specs=[
            pl.BlockSpec(memory_space=pltpu.SMEM),
            pl.BlockSpec(memory_space=pltpu.VMEM),
            pl.BlockSpec(memory_space=pltpu.VMEM),
        ],
        out_specs=pl.BlockSpec(memory_space=pltpu.VMEM),
        compiler_params=pltpu.CompilerParams(vmem_limit_bytes=24 * MIB),
        cost_estimate=pl.CostEstimate(flops=4 * 512 * 512 * 256, bytes_accessed=2 * MIB, transcendentals=0),
    )(core, kept, came)


def residual_kernel(blocks_ref, amplitudes_ref, kept_ref, sent_ref, joined):
    parts, rows, width = blocks_ref.shape
    ks = 4
    cs = width // ks

    @pl.when(pl.program_id(0) == 0)
    def _():
        for k in range(ks):
            for pair in range(parts // 2):
                at = k * parts * cs + pair * 2 * cs
                joined[:, at : at + 2 * cs] = jnp.concatenate(
                    [blocks_ref[2 * pair + i, :, k * cs : (k + 1) * cs] for i in range(2)], axis=1
                )

    total = lax.dot_general(
        joined[...], amplitudes_ref[...], (((1,), (1,)), ((), ())), preferred_element_type=F32
    )
    kept_ref[...] = total[: rows // 2]
    sent_ref[...] = total[rows // 2 :].astype(BF16)


def residual_partials(blocks, amplitudes, tile=512):
    parts, rows, width = blocks.shape
    local_rows, depth = amplitudes.shape
    return pl.pallas_call(
        residual_kernel,
        grid=(local_rows // tile,),
        out_shape=(
            jax.ShapeDtypeStruct((rows // 2, local_rows), F32),
            jax.ShapeDtypeStruct((rows // 2, local_rows), BF16),
        ),
        in_specs=[
            pl.BlockSpec((parts, rows, width), lambda m: (0, 0, 0)),
            pl.BlockSpec((tile, depth), lambda m: (m, 0)),
        ],
        out_specs=(
            pl.BlockSpec((rows // 2, tile), lambda m: (0, m)),
            pl.BlockSpec((rows // 2, tile), lambda m: (0, m)),
        ),
        scratch_shapes=[pltpu.VMEM((rows, depth), BF16)],
        compiler_params=pltpu.CompilerParams(vmem_limit_bytes=32 * MIB),
        cost_estimate=pl.CostEstimate(
            flops=2 * rows * local_rows * depth, bytes_accessed=24 * MIB, transcendentals=0
        ),
    )(blocks, amplitudes)


def per_device(amplitudes, occupied_factors, virtual_factors):
    kc_size = lax.axis_size("kc")
    ia_size = lax.axis_size("ia")
    chips = kc_size // 2
    core = lax.axis_index("kc") % 2
    same_core = [[2 * t + c for t in range(chips)] for c in range(2)]
    swap = [(i, i ^ 1) for i in range(kc_size)]
    depth, kj = occupied_factors.shape
    cb = virtual_factors.shape[1]

    payload = jnp.concatenate(
        [
            occupied_factors.reshape(depth, chips, kj // chips).transpose(1, 0, 2),
            jnp.broadcast_to(virtual_factors[None], (chips, depth, cb)),
        ],
        axis=1,
    )
    factors = lax.all_to_all(payload, "kc", 0, 0, axis_index_groups=same_core)
    occupied = factors[:, :depth].reshape(chips * depth, kj // chips)
    virtual = factors[:, depth:].reshape(chips * depth, cb)
    partial = lax.dot_general(
        occupied, virtual, (((0,), (0,)), ((), ())), preferred_element_type=F32
    ).reshape(2, kj // kc_size, cb)
    kept = lax.dynamic_index_in_dim(partial, core, 0, keepdims=False)
    came = lax.ppermute(lax.dynamic_index_in_dim(partial, 1 - core, 0, keepdims=False), "kc", swap)
    own = cycle_blocks(core[None], kept, came)

    blocks = lax.all_to_all(jnp.broadcast_to(own[None], (ia_size,) + own.shape), "ia", 0, 0)

    kept, sent = residual_partials(blocks, amplitudes)
    came = lax.ppermute(sent, "kc", swap)
    chip_sums = (kept + came.astype(F32)).astype(BF16)
    shares = lax.all_to_all(
        chip_sums.reshape(chips, O * BW // kc_size, -1), "kc", 0, 0, axis_index_groups=same_core
    )
    return jnp.sum(shares.astype(F32), axis=0).T


def solution(mesh):
    placed = (P("ia", "kc"), P("kc", None), P("kc", "ia"))
    return jax.shard_map(
        per_device, mesh=mesh, in_specs=placed, out_specs=P("ia", "kc"), check_vma=False
    )
```

```python
import functools

import jax
import jax.numpy as jnp
from jax import lax
from jax.experimental import pallas as pl
from jax.experimental.pallas import tpu as pltpu
from jax.sharding import PartitionSpec as P

O = 64
V = 512
BW = 8
F32 = jnp.float32
BF16 = jnp.bfloat16
MIB = 1 << 20
SMEM = pl.BlockSpec(memory_space=pltpu.SMEM)
VMEM = pl.BlockSpec(memory_space=pltpu.VMEM)
HBM = pl.BlockSpec(memory_space=pltpu.HBM)

SLOTS = ((1, 3), (5, 7), (2, 6), (4, 4))


def call(kernel, out_shape, n_scalars, n_arrays, scratch=(), flops=0, moved=0, limit=8):
    single = not isinstance(out_shape, tuple)
    return pl.pallas_call(
        kernel,
        out_shape=out_shape,
        in_specs=[SMEM] * n_scalars + [VMEM] * n_arrays,
        out_specs=VMEM if single else tuple(VMEM for _ in out_shape),
        scratch_shapes=list(scratch),
        compiler_params=pltpu.CompilerParams(vmem_limit_bytes=limit * MIB),
        cost_estimate=pl.CostEstimate(flops=flops, bytes_accessed=moved, transcendentals=0),
    )


def payload_kernel(occupied_ref, virtual_ref, out_ref, held, virtual, sems):
    chips = out_ref.shape[0]
    depth, cb = virtual_ref.shape
    first = pltpu.make_async_copy(virtual_ref, virtual, sems.at[0, chips])
    first.start()
    came = [
        pltpu.make_async_copy(occupied_ref.at[:, pl.ds(t * cb, cb)], held.at[t], sems.at[0, t])
        for t in range(chips)
    ]
    for copy in came:
        copy.start()
    first.wait()
    out = [
        pltpu.make_async_copy(virtual, out_ref.at[t, pl.ds(depth, depth)], sems.at[1, t])
        for t in range(chips)
    ]
    for copy in out:
        copy.start()
    for t in range(chips):
        came[t].wait()
        out.append(pltpu.make_async_copy(held.at[t], out_ref.at[t, pl.ds(0, depth)], sems.at[2, t]))
        out[-1].start()
    for copy in out:
        copy.wait()


def integrals_kernel(place_ref, factors_ref, kept_ref, sent_ref, total):
    sources, two_depth, cb = factors_ref.shape
    depth = two_depth // 2
    half = kept_ref.shape[0]
    occupied = factors_ref[:, :depth].reshape(sources * depth, cb)
    virtual = factors_ref[:, depth:].reshape(sources * depth, cb)
    total[...] = lax.dot_general(
        occupied, virtual, (((0,), (0,)), ((), ())), preferred_element_type=F32
    )
    core = place_ref[1]
    kept_ref[...] = total[pl.ds(pl.multiple_of(core * half, half), half), :]
    sent_ref[...] = total[pl.ds(pl.multiple_of((1 - core) * half, half), half), :]


def block_kernel(place_ref, kept_ref, came_ref, out_ref):
    kj, cb = kept_ref.shape
    ks = kj // O
    cs = cb // BW
    rows = O * BW
    integrals = (kept_ref[...] + came_ref[...]).astype(BF16)
    source = lax.broadcasted_iota(jnp.int32, (cb, cb), 0)
    target = lax.broadcasted_iota(jnp.int32, (cb, cb), 1)
    move = jnp.where(source == (target % cs) * BW + target // cs, 1.0, 0.0).astype(BF16)
    by_b = jnp.dot(integrals, move, preferred_element_type=F32).astype(BF16)
    stacked = jnp.concatenate(
        [
            jnp.concatenate(
                [by_b[k * O : (k + 1) * O, b * cs : (b + 1) * cs] for b in range(BW)], axis=0
            )
            for k in range(ks)
        ],
        axis=1,
    )
    row = lax.broadcasted_iota(jnp.int32, (rows, 1), 0)
    chunk = row // 256
    within = row % 128
    sender = place_ref[1] ^ ((row // 128) % 2)
    first = chunk == 0
    paired = first | (within < 64)
    slot = jnp.where(
        first,
        1 + 2 * sender + 4 * (within // 64),
        jnp.where(within < 64, 2 + 4 * sender, jnp.where(within < 96, 4, 0)),
    )
    core = jnp.where(paired, sender ^ ((within // 32) % 2), sender)
    j = (place_ref[0] ^ slot) * 8 + core * 4 + (within % 32) // BW
    wanted = (within % BW) * O + j
    source = lax.broadcasted_iota(jnp.int32, (rows, rows), 1)
    move = jnp.where(source == wanted, 1.0, 0.0).astype(BF16)
    out_ref[...] = jnp.dot(move, stacked, preferred_element_type=F32).astype(BF16)


def join(mine, refs, rows, staged, joined):
    width = refs[0].shape[1]
    ks = 4
    cs = width // ks
    for d, ref in enumerate(refs):
        staged[mine ^ d] = ref[rows, :]
    for k in range(ks):
        for pair in range(2):
            at = k * width + pair * 2 * cs
            joined[:, at : at + 2 * cs] = jnp.concatenate(
                [staged[2 * pair + i, :, k * cs : (k + 1) * cs] for i in range(2)], axis=1
            )


def columns_of(x, amplitudes_ref, into, tiles, sems):
    width = into.shape[1] // 4
    tile = into.shape[0] // tiles
    copies = []
    for m in range(tiles):
        for k in range(4):
            at = pl.multiple_of(k * 2 * width + x * width, width)
            rows = pl.ds(m * tile, tile)
            copies.append(
                pltpu.make_async_copy(
                    amplitudes_ref.at[rows, pl.ds(at, width)],
                    into.at[rows, pl.ds(k * width, width)],
                    sems.at[m, k],
                )
            )
    return copies


def far_columns_kernel(place_ref, amplitudes_ref, far_ref, sems):
    copies = columns_of(1 - place_ref[2], amplitudes_ref, far_ref, 2, sems)
    for copy in copies:
        copy.start()
    for copy in copies:
        copy.wait()


def near_kernel(tile, place_ref, b0, b1, b2, b3, amplitudes_ref, out_ref, held, staged, joined, sems):
    tiles = amplitudes_ref.shape[0] // tile
    copies = columns_of(place_ref[2], amplitudes_ref, held, tiles, sems)
    for copy in copies:
        copy.start()
    join(place_ref[3], (b0, b1, b2, b3), slice(None), staged, joined)
    for m in range(tiles):
        for copy in copies[4 * m : 4 * m + 4]:
            copy.wait()
        columns = slice(m * tile, (m + 1) * tile)
        out_ref[:, columns] = lax.dot_general(
            joined[...], held[columns, :], (((1,), (1,)), ((), ())), preferred_element_type=F32
        )


def far_kernel(tile, lo, place_ref, b0, b1, b2, b3, amplitudes_ref, near_ref, kept_ref, sent_ref, staged, joined):
    rows = joined.shape[0]
    half = rows // 2
    join(place_ref[3], (b0, b1, b2, b3), slice(lo, lo + rows), staged, joined)
    for m in range(amplitudes_ref.shape[0] // tile):
        columns = slice(m * tile, (m + 1) * tile)
        total = near_ref[lo : lo + rows, columns] + lax.dot_general(
            joined[...], amplitudes_ref[columns, :], (((1,), (1,)), ((), ())), preferred_element_type=F32
        )
        kept_ref[:, columns] = total[:half]
        sent_ref[:, columns] = total[half:].astype(BF16)


def per_device(amplitudes, occupied_factors, virtual_factors):
    kc_size = lax.axis_size("kc")
    ia_size = lax.axis_size("ia")
    chips = kc_size // 2
    kc = lax.axis_index("kc")
    ia = lax.axis_index("ia")
    place = jnp.stack([kc // 2, kc % 2, ia // 4, ia % 4]).astype(jnp.int32)
    same_core = [[2 * t + c for t in range(chips)] for c in range(2)]
    swap = [(i, i ^ 1) for i in range(kc_size)]
    depth, kj = occupied_factors.shape
    cb = virtual_factors.shape[1]
    local_rows, width = amplitudes.shape
    rows = O * BW
    share = rows // kc_size

    def over_ia(array, bits):
        return lax.ppermute(array, "ia", [(i, i ^ bits) for i in range(ia_size)])

    payload = pl.pallas_call(
        payload_kernel,
        out_shape=jax.ShapeDtypeStruct((chips, 2 * depth, cb), BF16),
        in_specs=[HBM, HBM],
        out_specs=HBM,
        scratch_shapes=[
            pltpu.VMEM((chips, depth, cb), BF16),
            pltpu.VMEM((depth, cb), BF16),
            pltpu.SemaphoreType.DMA((3, chips + 1)),
        ],
        compiler_params=pltpu.CompilerParams(vmem_limit_bytes=60 * MIB),
        cost_estimate=pl.CostEstimate(flops=0, bytes_accessed=4 * MIB, transcendentals=0),
    )(occupied_factors, virtual_factors)
    factors = lax.all_to_all(payload, "kc", 0, 0, axis_index_groups=same_core)
    held_far = pl.pallas_call(
        far_columns_kernel,
        out_shape=jax.ShapeDtypeStruct((local_rows, width // 2), BF16),
        in_specs=[SMEM, HBM],
        out_specs=VMEM,
        scratch_shapes=[pltpu.SemaphoreType.DMA((2, 4))],
        compiler_params=pltpu.CompilerParams(vmem_limit_bytes=40 * MIB),
        cost_estimate=pl.CostEstimate(flops=0, bytes_accessed=16 * MIB, transcendentals=0),
    )(place, amplitudes)
    factors, held_far = lax.optimization_barrier((factors, held_far))
    half = jax.ShapeDtypeStruct((kj // kc_size, cb), F32)
    kept, sent = call(
        integrals_kernel,
        (half, half),
        1,
        1,
        scratch=[pltpu.VMEM((kj // chips, cb), F32)],
        flops=2 * chips * depth * cb * cb,
        moved=3 * MIB,
    )(place, factors)
    came = lax.ppermute(sent, "kc", swap)
    own = call(
        block_kernel,
        jax.ShapeDtypeStruct((rows, width // ia_size), BF16),
        1,
        2,
        flops=4 * 512 * 512 * 256,
        moved=2 * MIB,
    )(place, kept, came)

    across = over_ia(own, 4)
    own1 = over_ia(own, 1)
    own3 = over_ia(own, 3)
    own2 = over_ia(own, 2)
    across1 = over_ia(across, 1)
    across3 = over_ia(across, 3)
    across2 = over_ia(own2, 4)

    tile = 1024
    flops = rows * local_rows * width
    near = pl.pallas_call(
        functools.partial(near_kernel, tile),
        out_shape=jax.ShapeDtypeStruct((rows, local_rows), F32),
        in_specs=[SMEM] + [VMEM] * 4 + [HBM],
        out_specs=VMEM,
        scratch_shapes=[
            pltpu.VMEM((local_rows, width // 2), BF16),
            pltpu.VMEM((4, rows, width // ia_size), BF16),
            pltpu.VMEM((rows, width // 2), BF16),
            pltpu.SemaphoreType.DMA((local_rows // tile, 4)),
        ],
        compiler_params=pltpu.CompilerParams(vmem_limit_bytes=36 * MIB),
        cost_estimate=pl.CostEstimate(flops=flops, bytes_accessed=17 * MIB, transcendentals=0),
    )(place, own, own1, own2, own3, amplitudes)

    def far(lo):
        part = rows // 4
        return call(
            functools.partial(far_kernel, tile, lo),
            (
                jax.ShapeDtypeStruct((part, local_rows), F32),
                jax.ShapeDtypeStruct((part, local_rows), BF16),
            ),
            1,
            6,
            scratch=[
                pltpu.VMEM((4, 2 * part, width // ia_size), BF16),
                pltpu.VMEM((2 * part, width // 2), BF16),
            ],
            flops=flops // 2,
            moved=12 * MIB,
        )(place, across, across1, across2, across3, held_far, near)

    def to_slot(array, bits):
        pairs = [(2 * t + c, 2 * (t ^ bits[c]) + c) for t in range(chips) for c in range(2)]
        return lax.ppermute(array, "kc", pairs)

    kept_a, sent_a = far(0)
    kept_b, sent_b = far(rows // 2)
    sums_a = kept_a + lax.ppermute(sent_a, "kc", swap).astype(F32)
    got0 = to_slot(sums_a[: 2 * share].astype(BF16), SLOTS[0])
    got1 = to_slot(sums_a[2 * share :].astype(BF16), SLOTS[1])
    sums_b = kept_b + lax.ppermute(sent_b, "kc", swap).astype(F32)
    got2 = to_slot(sums_b[: 2 * share].astype(BF16), SLOTS[2])
    got3 = to_slot(sums_b[2 * share : 3 * share].astype(BF16), SLOTS[3])
    got0, got1, got2, got3 = lax.optimization_barrier((got0, got1, got2, got3))
    got0, got1, got2, got3 = (got.astype(F32) for got in (got0, got1, got2, got3))
    mine = sums_b[3 * share :] + got0[:share] + got1[:share] + got2[:share] + got3
    other = got0[share:] + got1[share:] + got2[share:]
    return (mine + lax.ppermute(other, "kc", swap)).T


def solution(mesh):
    placed = (P("ia", "kc"), P("kc", None), P("kc", "ia"))
    return jax.shard_map(
        per_device, mesh=mesh, in_specs=placed, out_specs=P("ia", "kc"), check_vma=False
    )
```

```python
import functools

import jax
import jax.numpy as jnp
from jax import lax
from jax.experimental import pallas as pl
from jax.experimental.pallas import tpu as pltpu
from jax.sharding import PartitionSpec as P

O = 64
V = 512
BW = 8
F32 = jnp.float32
BF16 = jnp.bfloat16
MIB = 1 << 20
SMEM = pl.BlockSpec(memory_space=pltpu.SMEM)
VMEM = pl.BlockSpec(memory_space=pltpu.VMEM)
HBM = pl.BlockSpec(memory_space=pltpu.HBM)

SLOTS = ((5, 7), (2, 6), (1, 3), (4, 4))


def call(kernel, out_shape, n_scalars, n_arrays, scratch=(), flops=0, moved=0, limit=8):
    single = not isinstance(out_shape, tuple)
    return pl.pallas_call(
        kernel,
        out_shape=out_shape,
        in_specs=[SMEM] * n_scalars + [VMEM] * n_arrays,
        out_specs=VMEM if single else tuple(VMEM for _ in out_shape),
        scratch_shapes=list(scratch),
        compiler_params=pltpu.CompilerParams(vmem_limit_bytes=limit * MIB),
        cost_estimate=pl.CostEstimate(flops=flops, bytes_accessed=moved, transcendentals=0),
    )


def payload_kernel(occupied_ref, virtual_ref, out_ref, held, virtual, sems):
    chips = out_ref.shape[0]
    depth, cb = virtual_ref.shape
    first = pltpu.make_async_copy(virtual_ref, virtual, sems.at[0, chips])
    first.start()
    came = [
        pltpu.make_async_copy(occupied_ref.at[:, pl.ds(t * cb, cb)], held.at[t], sems.at[0, t])
        for t in range(chips)
    ]
    for copy in came:
        copy.start()
    first.wait()
    out = [
        pltpu.make_async_copy(virtual, out_ref.at[t, pl.ds(depth, depth)], sems.at[1, t])
        for t in range(chips)
    ]
    for copy in out:
        copy.start()
    for t in range(chips):
        came[t].wait()
        out.append(pltpu.make_async_copy(held.at[t], out_ref.at[t, pl.ds(0, depth)], sems.at[2, t]))
        out[-1].start()
    for copy in out:
        copy.wait()


def integrals_kernel(place_ref, factors_ref, kept_ref, sent_ref, total):
    sources, two_depth, cb = factors_ref.shape
    depth = two_depth // 2
    half = kept_ref.shape[0]
    occupied = factors_ref[:, :depth].reshape(sources * depth, cb)
    virtual = factors_ref[:, depth:].reshape(sources * depth, cb)
    total[...] = lax.dot_general(
        occupied, virtual, (((0,), (0,)), ((), ())), preferred_element_type=F32
    )
    core = place_ref[1]
    kept_ref[...] = total[pl.ds(pl.multiple_of(core * half, half), half), :]
    sent_ref[...] = total[pl.ds(pl.multiple_of((1 - core) * half, half), half), :]


def block_kernel(place_ref, kept_ref, came_ref, out_ref):
    kj, cb = kept_ref.shape
    ks = kj // O
    cs = cb // BW
    rows = O * BW
    integrals = (kept_ref[...] + came_ref[...]).astype(BF16)
    source = lax.broadcasted_iota(jnp.int32, (cb, cb), 0)
    target = lax.broadcasted_iota(jnp.int32, (cb, cb), 1)
    move = jnp.where(source == (target % cs) * BW + target // cs, 1.0, 0.0).astype(BF16)
    by_b = jnp.dot(integrals, move, preferred_element_type=F32).astype(BF16)
    stacked = jnp.concatenate(
        [
            jnp.concatenate(
                [by_b[k * O : (k + 1) * O, b * cs : (b + 1) * cs] for b in range(BW)], axis=0
            )
            for k in range(ks)
        ],
        axis=1,
    )
    row = lax.broadcasted_iota(jnp.int32, (rows, 1), 0)
    chunk = row // 256
    within = row % 128
    sender = place_ref[1] ^ ((row // 128) % 2)
    first = chunk == 0
    paired = first | (within < 64)
    slot = jnp.where(
        first,
        jnp.where(within < 64, 5 + 2 * sender, 2 + 4 * sender),
        jnp.where(within < 64, 1 + 2 * sender, jnp.where(within < 96, 4, 0)),
    )
    core = jnp.where(paired, sender ^ ((within // 32) % 2), sender)
    j = (place_ref[0] ^ slot) * 8 + core * 4 + (within % 32) // BW
    wanted = (within % BW) * O + j
    source = lax.broadcasted_iota(jnp.int32, (rows, rows), 1)
    move = jnp.where(source == wanted, 1.0, 0.0).astype(BF16)
    out_ref[...] = jnp.dot(move, stacked, preferred_element_type=F32).astype(BF16)


def join(mine, refs, rows, staged, joined):
    width = refs[0].shape[1]
    ks = 4
    cs = width // ks
    for d, ref in enumerate(refs):
        staged[mine ^ d] = ref[rows, :]
    for k in range(ks):
        for pair in range(2):
            at = k * width + pair * 2 * cs
            joined[:, at : at + 2 * cs] = jnp.concatenate(
                [staged[2 * pair + i, :, k * cs : (k + 1) * cs] for i in range(2)], axis=1
            )


def columns_of(x, amplitudes_ref, into, tiles, sems):
    width = into.shape[1] // 4
    tile = into.shape[0] // tiles
    copies = []
    for m in range(tiles):
        for k in range(4):
            at = pl.multiple_of(k * 2 * width + x * width, width)
            rows = pl.ds(m * tile, tile)
            copies.append(
                pltpu.make_async_copy(
                    amplitudes_ref.at[rows, pl.ds(at, width)],
                    into.at[rows, pl.ds(k * width, width)],
                    sems.at[m, k],
                )
            )
    return copies


def columns_kernel(far, place_ref, amplitudes_ref, out_ref, sems):
    copies = columns_of(place_ref[2] ^ far, amplitudes_ref, out_ref, 2, sems)
    for copy in copies:
        copy.start()
    for copy in copies:
        copy.wait()


def near_kernel(tile, place_ref, b0, b1, b2, b3, held_ref, out_ref, staged, joined):
    join(place_ref[3], (b0, b1, b2, b3), slice(None), staged, joined)
    for m in range(held_ref.shape[0] // tile):
        columns = slice(m * tile, (m + 1) * tile)
        out_ref[:, columns] = lax.dot_general(
            joined[...], held_ref[columns, :], (((1,), (1,)), ((), ())), preferred_element_type=F32
        )


def far_kernel(tile, lo, place_ref, b0, b1, b2, b3, amplitudes_ref, near_ref, kept_ref, sent_ref, staged, joined):
    rows = joined.shape[0]
    half = rows // 2
    join(place_ref[3], (b0, b1, b2, b3), slice(lo, lo + rows), staged, joined)
    for m in range(amplitudes_ref.shape[0] // tile):
        columns = slice(m * tile, (m + 1) * tile)
        total = near_ref[lo : lo + rows, columns] + lax.dot_general(
            joined[...], amplitudes_ref[columns, :], (((1,), (1,)), ((), ())), preferred_element_type=F32
        )
        kept_ref[:, columns] = total[:half]
        sent_ref[:, columns] = total[half:].astype(BF16)


def per_device(amplitudes, occupied_factors, virtual_factors):
    kc_size = lax.axis_size("kc")
    ia_size = lax.axis_size("ia")
    chips = kc_size // 2
    kc = lax.axis_index("kc")
    ia = lax.axis_index("ia")
    place = jnp.stack([kc // 2, kc % 2, ia // 4, ia % 4]).astype(jnp.int32)
    same_core = [[2 * t + c for t in range(chips)] for c in range(2)]
    swap = [(i, i ^ 1) for i in range(kc_size)]
    depth, kj = occupied_factors.shape
    cb = virtual_factors.shape[1]
    local_rows, width = amplitudes.shape
    rows = O * BW
    share = rows // kc_size

    def over_ia(array, bits):
        return lax.ppermute(array, "ia", [(i, i ^ bits) for i in range(ia_size)])

    payload = pl.pallas_call(
        payload_kernel,
        out_shape=jax.ShapeDtypeStruct((chips, 2 * depth, cb), BF16),
        in_specs=[HBM, HBM],
        out_specs=HBM,
        scratch_shapes=[
            pltpu.VMEM((chips, depth, cb), BF16),
            pltpu.VMEM((depth, cb), BF16),
            pltpu.SemaphoreType.DMA((3, chips + 1)),
        ],
        compiler_params=pltpu.CompilerParams(vmem_limit_bytes=60 * MIB),
        cost_estimate=pl.CostEstimate(flops=0, bytes_accessed=4 * MIB, transcendentals=0),
    )(occupied_factors, virtual_factors)
    factors = lax.all_to_all(payload, "kc", 0, 0, axis_index_groups=same_core)
    def columns(far, where):
        return pl.pallas_call(
            functools.partial(columns_kernel, far),
            out_shape=jax.ShapeDtypeStruct((local_rows, width // 2), BF16),
            in_specs=[SMEM, HBM],
            out_specs=VMEM,
            scratch_shapes=[pltpu.SemaphoreType.DMA((2, 4))],
            compiler_params=pltpu.CompilerParams(vmem_limit_bytes=36 * MIB),
            cost_estimate=pl.CostEstimate(flops=0, bytes_accessed=16 * MIB, transcendentals=0),
        )(where, amplitudes)

    held_far = columns(1, place)
    factors, held_far = lax.optimization_barrier((factors, held_far))
    half = jax.ShapeDtypeStruct((kj // kc_size, cb), F32)
    kept, sent = call(
        integrals_kernel,
        (half, half),
        1,
        1,
        scratch=[pltpu.VMEM((kj // chips, cb), F32)],
        flops=2 * chips * depth * cb * cb,
        moved=3 * MIB,
    )(place, factors)
    came = lax.ppermute(sent, "kc", swap)
    own = call(
        block_kernel,
        jax.ShapeDtypeStruct((rows, width // ia_size), BF16),
        1,
        2,
        flops=4 * 512 * 512 * 256,
        moved=2 * MIB,
    )(place, kept, came)

    near_place, _ = lax.optimization_barrier((place, own))
    across = over_ia(own, 4)
    own1 = over_ia(own, 1)
    own3 = over_ia(own, 3)
    own2 = over_ia(own, 2)
    across1 = over_ia(across, 1)
    across3 = over_ia(across, 3)
    across2 = over_ia(own2, 4)

    tile = 1024
    flops = rows * local_rows * width
    held_near = columns(0, near_place)
    near = call(
        functools.partial(near_kernel, tile),
        jax.ShapeDtypeStruct((rows, local_rows), F32),
        1,
        5,
        scratch=[pltpu.VMEM((4, rows, width // ia_size), BF16), pltpu.VMEM((rows, width // 2), BF16)],
        flops=flops,
        moved=17 * MIB,
    )(place, own, own1, own2, own3, held_near)

    def far(lo):
        part = rows // 4
        return call(
            functools.partial(far_kernel, tile, lo),
            (
                jax.ShapeDtypeStruct((part, local_rows), F32),
                jax.ShapeDtypeStruct((part, local_rows), BF16),
            ),
            1,
            6,
            scratch=[
                pltpu.VMEM((4, 2 * part, width // ia_size), BF16),
                pltpu.VMEM((2 * part, width // 2), BF16),
            ],
            flops=flops // 2,
            moved=12 * MIB,
        )(place, across, across1, across2, across3, held_far, near)

    def to_slot(array, bits):
        pairs = [(2 * t + c, 2 * (t ^ bits[c]) + c) for t in range(chips) for c in range(2)]
        return lax.ppermute(array, "kc", pairs)

    kept_a, sent_a = far(0)
    kept_b, sent_b = far(rows // 2)
    sums_a = kept_a + lax.ppermute(sent_a, "kc", swap).astype(F32)
    got0 = to_slot(sums_a[: 2 * share].astype(BF16), SLOTS[0])
    got1 = to_slot(sums_a[2 * share :].astype(BF16), SLOTS[1])
    sums_b = kept_b + lax.ppermute(sent_b, "kc", swap).astype(F32)
    got2 = to_slot(sums_b[: 2 * share].astype(BF16), SLOTS[2])
    got3 = to_slot(sums_b[2 * share : 3 * share].astype(BF16), SLOTS[3])
    mine = sums_b[3 * share :] + got0[:share].astype(F32) + got1[:share].astype(F32) + got3.astype(F32)
    other = got0[share:].astype(F32) + got1[share:].astype(F32)
    mine, other, got2 = lax.optimization_barrier((mine, other, got2))
    other = other + got2[share:].astype(F32)
    return (mine + got2[:share].astype(F32) + lax.ppermute(other, "kc", swap)).T


def solution(mesh):
    placed = (P("ia", "kc"), P("kc", None), P("kc", "ia"))
    return jax.shard_map(
        per_device, mesh=mesh, in_specs=placed, out_specs=P("ia", "kc"), check_vma=False
    )
```

```python
import functools

import jax
import jax.numpy as jnp
from jax import lax
from jax.experimental import pallas as pl
from jax.experimental.pallas import tpu as pltpu
from jax.sharding import PartitionSpec as P

O = 64
V = 512
BW = 8
F32 = jnp.float32
BF16 = jnp.bfloat16
MIB = 1 << 20
SMEM = pl.BlockSpec(memory_space=pltpu.SMEM)
VMEM = pl.BlockSpec(memory_space=pltpu.VMEM)
HBM = pl.BlockSpec(memory_space=pltpu.HBM)

SLOTS = ((5, 7), (2, 6), (1, 3), (4, 4))


def call(kernel, out_shape, n_scalars, n_arrays, scratch=(), flops=0, moved=0, limit=8):
    single = not isinstance(out_shape, tuple)
    return pl.pallas_call(
        kernel,
        out_shape=out_shape,
        in_specs=[SMEM] * n_scalars + [VMEM] * n_arrays,
        out_specs=VMEM if single else tuple(VMEM for _ in out_shape),
        scratch_shapes=list(scratch),
        compiler_params=pltpu.CompilerParams(vmem_limit_bytes=limit * MIB),
        cost_estimate=pl.CostEstimate(flops=flops, bytes_accessed=moved, transcendentals=0),
    )


def payload_kernel(occupied_ref, virtual_ref, out_ref, held, virtual, sems):
    chips = out_ref.shape[0]
    depth, cb = virtual_ref.shape
    first = pltpu.make_async_copy(virtual_ref, virtual, sems.at[0, chips])
    first.start()
    came = [
        pltpu.make_async_copy(occupied_ref.at[:, pl.ds(t * cb, cb)], held.at[t], sems.at[0, t])
        for t in range(chips)
    ]
    for copy in came:
        copy.start()
    first.wait()
    out = [
        pltpu.make_async_copy(virtual, out_ref.at[t, pl.ds(depth, depth)], sems.at[1, t])
        for t in range(chips)
    ]
    for copy in out:
        copy.start()
    for t in range(chips):
        came[t].wait()
        out.append(pltpu.make_async_copy(held.at[t], out_ref.at[t, pl.ds(0, depth)], sems.at[2, t]))
        out[-1].start()
    for copy in out:
        copy.wait()


def integrals_kernel(other, place_ref, factors_ref, out_ref):
    sources, two_depth, cb = factors_ref.shape
    depth = two_depth // 2
    half = out_ref.shape[0]
    at = pl.multiple_of((place_ref[1] ^ other) * half, half)
    occupied = factors_ref[:, :depth, pl.ds(at, half)].reshape(sources * depth, half)
    virtual = factors_ref[:, depth:].reshape(sources * depth, cb)
    out_ref[...] = lax.dot_general(
        occupied, virtual, (((0,), (0,)), ((), ())), preferred_element_type=F32
    )


def block_kernel(place_ref, kept_ref, came_ref, out_ref):
    kj, cb = kept_ref.shape
    ks = kj // O
    cs = cb // BW
    rows = O * BW
    integrals = (kept_ref[...] + came_ref[...]).astype(BF16)
    source = lax.broadcasted_iota(jnp.int32, (cb, cb), 0)
    target = lax.broadcasted_iota(jnp.int32, (1, cb), 1)
    move = jnp.where(source == (target % cs) * BW + target // cs, 1.0, 0.0).astype(BF16)
    by_b = jnp.dot(integrals, move, preferred_element_type=F32).astype(BF16)
    stacked = jnp.concatenate(
        [
            jnp.concatenate(
                [by_b[k * O : (k + 1) * O, b * cs : (b + 1) * cs] for b in range(BW)], axis=0
            )
            for k in range(ks)
        ],
        axis=1,
    )
    row = lax.broadcasted_iota(jnp.int32, (rows, 1), 0)
    chunk = row // 256
    within = row % 128
    sender = place_ref[1] ^ ((row // 128) % 2)
    first = chunk == 0
    paired = first | (within < 64)
    slot = jnp.where(
        first,
        jnp.where(within < 64, 5 + 2 * sender, 2 + 4 * sender),
        jnp.where(within < 64, 1 + 2 * sender, jnp.where(within < 96, 4, 0)),
    )
    core = jnp.where(paired, sender ^ ((within // 32) % 2), sender)
    j = (place_ref[0] ^ slot) * 8 + core * 4 + (within % 32) // BW
    wanted = (within % BW) * O + j
    source = lax.broadcasted_iota(jnp.int32, (rows, rows), 1)
    move = jnp.where(source == wanted, 1.0, 0.0).astype(BF16)
    out_ref[...] = jnp.dot(move, stacked, preferred_element_type=F32).astype(BF16)


def join(mine, refs, rows, staged, joined):
    width = refs[0].shape[1]
    ks = 4
    cs = width // ks
    for d, ref in enumerate(refs):
        staged[mine ^ d] = ref[rows, :]
    for k in range(ks):
        for pair in range(2):
            at = k * width + pair * 2 * cs
            joined[:, at : at + 2 * cs] = jnp.concatenate(
                [staged[2 * pair + i, :, k * cs : (k + 1) * cs] for i in range(2)], axis=1
            )


def columns_of(x, amplitudes_ref, into, tiles, sems):
    width = into.shape[1] // 4
    tile = into.shape[0] // tiles
    copies = []
    for m in range(tiles):
        for k in range(4):
            at = pl.multiple_of(k * 2 * width + x * width, width)
            rows = pl.ds(m * tile, tile)
            copies.append(
                pltpu.make_async_copy(
                    amplitudes_ref.at[rows, pl.ds(at, width)],
                    into.at[rows, pl.ds(k * width, width)],
                    sems.at[m, k],
                )
            )
    return copies


def columns_kernel(far, place_ref, amplitudes_ref, out_ref, sems):
    copies = columns_of(place_ref[2] ^ far, amplitudes_ref, out_ref, 2, sems)
    for copy in copies:
        copy.start()
    for copy in copies:
        copy.wait()


def near_kernel(tile, place_ref, b0, b1, b2, b3, held_ref, out_ref, staged, joined):
    join(place_ref[3], (b0, b1, b2, b3), slice(None), staged, joined)
    for m in range(held_ref.shape[0] // tile):
        columns = slice(m * tile, (m + 1) * tile)
        out_ref[:, columns] = lax.dot_general(
            joined[...], held_ref[columns, :], (((1,), (1,)), ((), ())), preferred_element_type=F32
        )


def far_kernel(tile, lo, place_ref, b0, b1, b2, b3, amplitudes_ref, near_ref, kept_ref, sent_ref, staged, joined):
    rows = joined.shape[0]
    half = rows // 2
    join(place_ref[3], (b0, b1, b2, b3), slice(lo, lo + rows), staged, joined)
    for m in range(amplitudes_ref.shape[0] // tile):
        columns = slice(m * tile, (m + 1) * tile)
        total = near_ref[lo : lo + rows, columns] + lax.dot_general(
            joined[...], amplitudes_ref[columns, :], (((1,), (1,)), ((), ())), preferred_element_type=F32
        )
        kept_ref[:, columns] = total[:half]
        sent_ref[:, columns] = total[half:].astype(BF16)


def per_device(amplitudes, occupied_factors, virtual_factors):
    kc_size = lax.axis_size("kc")
    ia_size = lax.axis_size("ia")
    chips = kc_size // 2
    kc = lax.axis_index("kc")
    ia = lax.axis_index("ia")
    place = jnp.stack([kc // 2, kc % 2, ia // 4, ia % 4]).astype(jnp.int32)
    same_core = [[2 * t + c for t in range(chips)] for c in range(2)]
    swap = [(i, i ^ 1) for i in range(kc_size)]
    depth, kj = occupied_factors.shape
    cb = virtual_factors.shape[1]
    local_rows, width = amplitudes.shape
    rows = O * BW
    share = rows // kc_size

    def over_ia(array, bits):
        return lax.ppermute(array, "ia", [(i, i ^ bits) for i in range(ia_size)])

    payload = pl.pallas_call(
        payload_kernel,
        out_shape=jax.ShapeDtypeStruct((chips, 2 * depth, cb), BF16),
        in_specs=[HBM, HBM],
        out_specs=HBM,
        scratch_shapes=[
            pltpu.VMEM((chips, depth, cb), BF16),
            pltpu.VMEM((depth, cb), BF16),
            pltpu.SemaphoreType.DMA((3, chips + 1)),
        ],
        compiler_params=pltpu.CompilerParams(vmem_limit_bytes=60 * MIB),
        cost_estimate=pl.CostEstimate(flops=0, bytes_accessed=4 * MIB, transcendentals=0),
    )(occupied_factors, virtual_factors)
    factors = lax.all_to_all(payload, "kc", 0, 0, axis_index_groups=same_core)
    def columns(far, where):
        return pl.pallas_call(
            functools.partial(columns_kernel, far),
            out_shape=jax.ShapeDtypeStruct((local_rows, width // 2), BF16),
            in_specs=[SMEM, HBM],
            out_specs=VMEM,
            scratch_shapes=[pltpu.SemaphoreType.DMA((2, 4))],
            compiler_params=pltpu.CompilerParams(vmem_limit_bytes=36 * MIB),
            cost_estimate=pl.CostEstimate(flops=0, bytes_accessed=16 * MIB, transcendentals=0),
        )(where, amplitudes)

    held_far = columns(1, place)
    factors, held_far = lax.optimization_barrier((factors, held_far))
    half = jax.ShapeDtypeStruct((kj // kc_size, cb), F32)
    sent, kept = (
        call(
            functools.partial(integrals_kernel, other),
            half,
            1,
            1,
            flops=chips * depth * cb * cb,
            moved=3 * MIB,
        )(place, factors)
        for other in (1, 0)
    )
    came = lax.ppermute(sent, "kc", swap)
    own = call(
        block_kernel,
        jax.ShapeDtypeStruct((rows, width // ia_size), BF16),
        1,
        2,
        flops=4 * 512 * 512 * 256,
        moved=2 * MIB,
    )(place, kept, came)

    near_place, _ = lax.optimization_barrier((place, own))
    across = over_ia(own, 4)
    own1 = over_ia(own, 1)
    own3 = over_ia(own, 3)
    own2 = over_ia(own, 2)
    across1 = over_ia(across, 1)
    across3 = over_ia(across, 3)
    across2 = over_ia(own2, 4)

    tile = 1024
    flops = rows * local_rows * width
    held_near = columns(0, near_place)
    near = call(
        functools.partial(near_kernel, tile),
        jax.ShapeDtypeStruct((rows, local_rows), F32),
        1,
        5,
        scratch=[pltpu.VMEM((4, rows, width // ia_size), BF16), pltpu.VMEM((rows, width // 2), BF16)],
        flops=flops,
        moved=17 * MIB,
    )(place, own, own1, own2, own3, held_near)

    def far(lo):
        part = rows // 4
        return call(
            functools.partial(far_kernel, tile, lo),
            (
                jax.ShapeDtypeStruct((part, local_rows), F32),
                jax.ShapeDtypeStruct((part, local_rows), BF16),
            ),
            1,
            6,
            scratch=[
                pltpu.VMEM((4, 2 * part, width // ia_size), BF16),
                pltpu.VMEM((2 * part, width // 2), BF16),
            ],
            flops=flops // 2,
            moved=12 * MIB,
        )(place, across, across1, across2, across3, held_far, near)

    def to_slot(array, bits):
        pairs = [(2 * t + c, 2 * (t ^ bits[c]) + c) for t in range(chips) for c in range(2)]
        return lax.ppermute(array, "kc", pairs)

    kept_a, sent_a = far(0)
    kept_b, sent_b = far(rows // 2)
    sums_a = kept_a + lax.ppermute(sent_a, "kc", swap).astype(F32)
    got0 = to_slot(sums_a[: 2 * share].astype(BF16), SLOTS[0])
    got1 = to_slot(sums_a[2 * share :].astype(BF16), SLOTS[1])
    sums_b = kept_b + lax.ppermute(sent_b, "kc", swap).astype(F32)
    got2 = to_slot(sums_b[: 2 * share].astype(BF16), SLOTS[2])
    got3 = to_slot(sums_b[2 * share : 3 * share].astype(BF16), SLOTS[3])
    mine = sums_b[3 * share :] + got0[:share].astype(F32) + got1[:share].astype(F32) + got3.astype(F32)
    other = got0[share:].astype(F32) + got1[share:].astype(F32)
    mine, other, got2 = lax.optimization_barrier((mine, other, got2))
    other = other + got2[share:].astype(F32)
    return (mine + got2[:share].astype(F32) + lax.ppermute(other, "kc", swap)).T


def solution(mesh):
    placed = (P("ia", "kc"), P("kc", None), P("kc", "ia"))
    return jax.shard_map(
        per_device, mesh=mesh, in_specs=placed, out_specs=P("ia", "kc"), check_vma=False
    )
```

```python
import functools

import jax
import jax.numpy as jnp
from jax import lax
from jax.experimental import pallas as pl
from jax.experimental.pallas import tpu as pltpu
from jax.sharding import PartitionSpec as P

O = 64
V = 512
BW = 8
F32 = jnp.float32
BF16 = jnp.bfloat16
MIB = 1 << 20
SMEM = pl.BlockSpec(memory_space=pltpu.SMEM)
VMEM = pl.BlockSpec(memory_space=pltpu.VMEM)
HBM = pl.BlockSpec(memory_space=pltpu.HBM)

SLOTS = ((5, 7), (4, 4), (2, 6), (1, 3))


def call(kernel, out_shape, n_scalars, n_arrays, scratch=(), flops=0, moved=0, limit=8):
    single = not isinstance(out_shape, tuple)
    return pl.pallas_call(
        kernel,
        out_shape=out_shape,
        in_specs=[SMEM] * n_scalars + [VMEM] * n_arrays,
        out_specs=VMEM if single else tuple(VMEM for _ in out_shape),
        scratch_shapes=list(scratch),
        compiler_params=pltpu.CompilerParams(vmem_limit_bytes=limit * MIB),
        cost_estimate=pl.CostEstimate(flops=flops, bytes_accessed=moved, transcendentals=0),
    )


def payload_kernel(occupied_ref, virtual_ref, out_ref, held, virtual, sems):
    chips = out_ref.shape[0]
    depth, cb = virtual_ref.shape
    first = pltpu.make_async_copy(virtual_ref, virtual, sems.at[0, chips])
    first.start()
    came = [
        pltpu.make_async_copy(occupied_ref.at[:, pl.ds(t * cb, cb)], held.at[t], sems.at[0, t])
        for t in range(chips)
    ]
    for copy in came:
        copy.start()
    first.wait()
    out = [
        pltpu.make_async_copy(virtual, out_ref.at[t, pl.ds(depth, depth)], sems.at[1, t])
        for t in range(chips)
    ]
    for copy in out:
        copy.start()
    for t in range(chips):
        came[t].wait()
        out.append(pltpu.make_async_copy(held.at[t], out_ref.at[t, pl.ds(0, depth)], sems.at[2, t]))
        out[-1].start()
    for copy in out:
        copy.wait()


def integrals_kernel(other, place_ref, factors_ref, out_ref):
    sources, two_depth, cb = factors_ref.shape
    depth = two_depth // 2
    half = out_ref.shape[0]
    at = pl.multiple_of((place_ref[1] ^ other) * half, half)
    occupied = factors_ref[:, :depth, pl.ds(at, half)].reshape(sources * depth, half)
    virtual = factors_ref[:, depth:].reshape(sources * depth, cb)
    out_ref[...] = lax.dot_general(
        occupied, virtual, (((0,), (0,)), ((), ())), preferred_element_type=F32
    )


def block_kernel(place_ref, kept_ref, came_ref, out_ref):
    kj, cb = kept_ref.shape
    ks = kj // O
    cs = cb // BW
    rows = O * BW
    integrals = (kept_ref[...] + came_ref[...]).astype(BF16)
    source = lax.broadcasted_iota(jnp.int32, (cb, cb), 0)
    target = lax.broadcasted_iota(jnp.int32, (1, cb), 1)
    move = jnp.where(source == (target % cs) * BW + target // cs, 1.0, 0.0).astype(BF16)
    by_b = jnp.dot(integrals, move, preferred_element_type=F32).astype(BF16)
    stacked = jnp.concatenate(
        [
            jnp.concatenate(
                [by_b[k * O : (k + 1) * O, b * cs : (b + 1) * cs] for b in range(BW)], axis=0
            )
            for k in range(ks)
        ],
        axis=1,
    )
    row = lax.broadcasted_iota(jnp.int32, (rows, 1), 0)
    chunk = row // 256
    within = row % 128
    sender = place_ref[1] ^ ((row // 128) % 2)
    first = chunk == 0
    paired = ~first | (within < 64)
    slot = jnp.where(
        first,
        jnp.where(within < 64, 5 + 2 * sender, jnp.where(within < 96, 4, 0)),
        jnp.where(within < 64, 2 + 4 * sender, 1 + 2 * sender),
    )
    core = jnp.where(paired, sender ^ ((within // 32) % 2), sender)
    j = (place_ref[0] ^ slot) * 8 + core * 4 + (within % 32) // BW
    wanted = (within % BW) * O + j
    source = lax.broadcasted_iota(jnp.int32, (rows, rows), 1)
    move = jnp.where(source == wanted, 1.0, 0.0).astype(BF16)
    out_ref[...] = jnp.dot(move, stacked, preferred_element_type=F32).astype(BF16)


def join(mine, refs, rows, staged, joined):
    width = refs[0].shape[1]
    ks = 4
    cs = width // ks
    for d, ref in enumerate(refs):
        staged[mine ^ d] = ref[rows, :]
    for k in range(ks):
        for pair in range(2):
            at = k * width + pair * 2 * cs
            joined[:, at : at + 2 * cs] = jnp.concatenate(
                [staged[2 * pair + i, :, k * cs : (k + 1) * cs] for i in range(2)], axis=1
            )


def columns_of(x, amplitudes_ref, into, tiles, sems):
    width = into.shape[1] // 4
    tile = into.shape[0] // tiles
    copies = []
    for m in range(tiles):
        for k in range(4):
            at = pl.multiple_of(k * 2 * width + x * width, width)
            rows = pl.ds(m * tile, tile)
            copies.append(
                pltpu.make_async_copy(
                    amplitudes_ref.at[rows, pl.ds(at, width)],
                    into.at[rows, pl.ds(k * width, width)],
                    sems.at[m, k],
                )
            )
    return copies


def columns_kernel(far, place_ref, amplitudes_ref, out_ref, sems):
    copies = columns_of(place_ref[2] ^ far, amplitudes_ref, out_ref, 2, sems)
    for copy in copies:
        copy.start()
    for copy in copies:
        copy.wait()


def near_kernel(tile, place_ref, b0, b1, b2, b3, held_ref, out_ref, staged, joined):
    join(place_ref[3], (b0, b1, b2, b3), slice(None), staged, joined)
    for m in range(held_ref.shape[0] // tile):
        columns = slice(m * tile, (m + 1) * tile)
        out_ref[:, columns] = lax.dot_general(
            joined[...], held_ref[columns, :], (((1,), (1,)), ((), ())), preferred_element_type=F32
        )


def far_kernel(tile, lo, place_ref, b0, b1, b2, b3, amplitudes_ref, near_ref, kept_ref, sent_ref, staged, joined):
    rows = joined.shape[0]
    half = rows // 2
    join(place_ref[3], (b0, b1, b2, b3), slice(lo, lo + rows), staged, joined)
    for m in range(amplitudes_ref.shape[0] // tile):
        columns = slice(m * tile, (m + 1) * tile)
        total = near_ref[lo : lo + rows, columns] + lax.dot_general(
            joined[...], amplitudes_ref[columns, :], (((1,), (1,)), ((), ())), preferred_element_type=F32
        )
        kept_ref[:, columns] = total[:half]
        sent_ref[:, columns] = total[half:].astype(BF16)


def per_device(amplitudes, occupied_factors, virtual_factors):
    kc_size = lax.axis_size("kc")
    ia_size = lax.axis_size("ia")
    chips = kc_size // 2
    kc = lax.axis_index("kc")
    ia = lax.axis_index("ia")
    place = jnp.stack([kc // 2, kc % 2, ia // 4, ia % 4]).astype(jnp.int32)
    same_core = [[2 * t + c for t in range(chips)] for c in range(2)]
    swap = [(i, i ^ 1) for i in range(kc_size)]
    depth, kj = occupied_factors.shape
    cb = virtual_factors.shape[1]
    local_rows, width = amplitudes.shape
    rows = O * BW
    share = rows // kc_size

    def over_ia(array, bits):
        return lax.ppermute(array, "ia", [(i, i ^ bits) for i in range(ia_size)])

    payload = pl.pallas_call(
        payload_kernel,
        out_shape=jax.ShapeDtypeStruct((chips, 2 * depth, cb), BF16),
        in_specs=[HBM, HBM],
        out_specs=HBM,
        scratch_shapes=[
            pltpu.VMEM((chips, depth, cb), BF16),
            pltpu.VMEM((depth, cb), BF16),
            pltpu.SemaphoreType.DMA((3, chips + 1)),
        ],
        compiler_params=pltpu.CompilerParams(vmem_limit_bytes=60 * MIB),
        cost_estimate=pl.CostEstimate(flops=0, bytes_accessed=4 * MIB, transcendentals=0),
    )(occupied_factors, virtual_factors)
    factors = lax.all_to_all(payload, "kc", 0, 0, axis_index_groups=same_core)
    def columns(far, where):
        return pl.pallas_call(
            functools.partial(columns_kernel, far),
            out_shape=jax.ShapeDtypeStruct((local_rows, width // 2), BF16),
            in_specs=[SMEM, HBM],
            out_specs=VMEM,
            scratch_shapes=[pltpu.SemaphoreType.DMA((2, 4))],
            compiler_params=pltpu.CompilerParams(vmem_limit_bytes=36 * MIB),
            cost_estimate=pl.CostEstimate(flops=0, bytes_accessed=16 * MIB, transcendentals=0),
        )(where, amplitudes)

    held_far = columns(1, place)
    factors, held_far = lax.optimization_barrier((factors, held_far))
    half = jax.ShapeDtypeStruct((kj // kc_size, cb), F32)
    sent, kept = (
        call(
            functools.partial(integrals_kernel, other),
            half,
            1,
            1,
            flops=chips * depth * cb * cb,
            moved=3 * MIB,
        )(place, factors)
        for other in (1, 0)
    )
    came = lax.ppermute(sent, "kc", swap)
    own = call(
        block_kernel,
        jax.ShapeDtypeStruct((rows, width // ia_size), BF16),
        1,
        2,
        flops=4 * 512 * 512 * 256,
        moved=2 * MIB,
    )(place, kept, came)

    near_place, _ = lax.optimization_barrier((place, own))
    across = over_ia(own, 4)
    own1 = over_ia(own, 1)
    own3 = over_ia(own, 3)
    own2 = over_ia(own, 2)
    across1 = over_ia(across, 1)
    across3 = over_ia(across, 3)
    across2 = over_ia(own2, 4)

    tile = 1024
    flops = rows * local_rows * width
    held_near = columns(0, near_place)
    near = call(
        functools.partial(near_kernel, tile),
        jax.ShapeDtypeStruct((rows, local_rows), F32),
        1,
        5,
        scratch=[pltpu.VMEM((4, rows, width // ia_size), BF16), pltpu.VMEM((rows, width // 2), BF16)],
        flops=flops,
        moved=17 * MIB,
    )(place, own, own1, own2, own3, held_near)

    def far(lo):
        part = rows // 4
        return call(
            functools.partial(far_kernel, tile, lo),
            (
                jax.ShapeDtypeStruct((part, local_rows), F32),
                jax.ShapeDtypeStruct((part, local_rows), BF16),
            ),
            1,
            6,
            scratch=[
                pltpu.VMEM((4, 2 * part, width // ia_size), BF16),
                pltpu.VMEM((2 * part, width // 2), BF16),
            ],
            flops=flops // 2,
            moved=12 * MIB,
        )(place, across, across1, across2, across3, held_far, near)

    def to_slot(array, bits):
        pairs = [(2 * t + c, 2 * (t ^ bits[c]) + c) for t in range(chips) for c in range(2)]
        return lax.ppermute(array, "kc", pairs)

    kept_a, sent_a = far(0)
    kept_b, sent_b = far(rows // 2)
    sums_a = kept_a + lax.ppermute(sent_a, "kc", swap).astype(F32)
    got0 = to_slot(sums_a[: 2 * share].astype(BF16), SLOTS[0])
    got1 = to_slot(sums_a[2 * share : 3 * share].astype(BF16), SLOTS[1])
    sums_b = kept_b + lax.ppermute(sent_b, "kc", swap).astype(F32)
    got2 = to_slot(sums_b[: 2 * share].astype(BF16), SLOTS[2])
    got3 = to_slot(sums_b[2 * share :].astype(BF16), SLOTS[3])
    mine = sums_a[3 * share :] + got0[:share].astype(F32) + got1.astype(F32) + got2[:share].astype(F32)
    other = got0[share:].astype(F32) + got2[share:].astype(F32)
    mine, other, got3 = lax.optimization_barrier((mine, other, got3))
    other = other + got3[share:].astype(F32)
    return (mine + got3[:share].astype(F32) + lax.ppermute(other, "kc", swap)).T


def solution(mesh):
    placed = (P("ia", "kc"), P("kc", None), P("kc", "ia"))
    return jax.shard_map(
        per_device, mesh=mesh, in_specs=placed, out_specs=P("ia", "kc"), check_vma=False
    )
```
